256 devices in a mesh: pix: 8 (over y, core), pos: 32 (over z, x).
Axes of the slice: x: 4, y: 4, z: 8, core: 2. Of those that a mesh axis runs over, the one named last changes fastest.
Arguments:
- stack: bfloat16 [16384, 2, 32768], P('pix', None, 'pos'), may hold values from -6 to 6
- omega: int32 [32768, 128], P('pos'), may hold values from -32768 to 32767
Outputs:
- basis: float32 [16384, 2, 128], P('pix')
- projected: float32 [128, 32768], P('pix', 'pos')
The draws below stay inside these ranges and needn't reach their ends.
All inputs are finite; a program needn't handle non-finite values.
Results may differ from the reference program's by a relative error of at most 0.0041.
Values may be sent and summed in bfloat16 or wider, within the bound.
A program may use at most 64 MiB of HBM per device.

```python
import math
import jax
import jax.numpy as jnp
from jax import lax

K = 128
PIXELS = 16384
POSITIONS = 32768


def draw_stack(key, part):
    key = jax.random.fold_in(key, 11)
    values = jax.random.normal(key, (PIXELS, 2, POSITIONS), jnp.float32)
    values = jnp.clip(values, -6.0, 6.0)
    return values.astype(jnp.bfloat16)


def with_ends(drawn, own_key, least, largest):
    extent = drawn.shape
    spot = [jax.random.randint(jax.random.fold_in(own_key, axis), (), 0, extent[axis]) for axis in range(len(extent))]
    drawn = drawn.at[tuple(spot)].set(least)
    longest = extent.index(max(extent))
    spot[longest] = (spot[longest] + 1) % extent[longest]
    return drawn.at[tuple(spot)].set(largest)


def setup_inputs(seed: int = 0) -> dict:
    key_of = jax.random.split(jax.random.key(seed), 3)
    stack = draw_stack(jax.random.fold_in(key_of[2], 71), 0)
    omega = with_ends(jax.random.randint(key_of[1], (POSITIONS, K), -32768, 32768), jax.random.fold_in(key_of[1], 1), -32768, 32767).astype(jnp.int32)
    return {"stack": stack, "omega": omega}


def reference(stack, omega):
    matrix = stack.reshape(2 * PIXELS, POSITIONS)
    test = (omega.astype(jnp.float32) / 32768.0).astype(jnp.bfloat16)
    first = jnp.dot(matrix.astype(jnp.float32), test.astype(jnp.float32), preferred_element_type=jnp.float32).astype(jnp.bfloat16)
    back = lax.dot_general(matrix.astype(jnp.float32), first.astype(jnp.float32), (((0,), (0,)), ((), ())), preferred_element_type=jnp.float32).astype(jnp.bfloat16)
    sketch = jnp.dot(matrix.astype(jnp.float32), back.astype(jnp.float32), preferred_element_type=jnp.float32)
    gram = lax.dot_general(sketch.astype(jnp.float32), sketch.astype(jnp.float32), (((0,), (0,)), ((), ())), precision=lax.Precision.HIGHEST, preferred_element_type=jnp.float32)
    lower = jnp.linalg.cholesky(gram)
    inverse = lax.linalg.triangular_solve(lower, jnp.eye(K, dtype=lower.dtype), left_side=True, lower=True)
    q_full = jnp.dot(sketch.astype(jnp.float32), inverse.T.astype(jnp.float32), precision=lax.Precision.HIGHEST, preferred_element_type=jnp.float32)
    basis = (q_full * math.sqrt(2.0 * PIXELS)).reshape(PIXELS, 2, K)
    q_low = q_full.astype(jnp.bfloat16)
    projected = lax.dot_general(q_low.astype(jnp.float32), matrix.astype(jnp.float32), (((0,), (0,)), ((), ())), preferred_element_type=jnp.float32)
    return (basis, projected)
```

```python
import math

import jax
import jax.numpy as jnp
from jax import lax
from jax.experimental import pallas as pl
from jax.experimental.pallas import tpu as pltpu
from jax.sharding import PartitionSpec as P

MESH = pl.DeviceIdType.MESH
K = 128
NX = 4
NZ = 8
NP = 8
ROWS = 4096
COLS = 1024
BLOCK = ROWS // NX
HALF = BLOCK // 2
CHUNK = BLOCK // NZ
FAR_FIRST = (4, 3, 5, 2, 6, 1, 7)
F32 = jnp.float32
BF16 = jnp.bfloat16


def contract(left, right, a, b):
    return lax.dot_general(left, right, (((a,), (b,)), ((), ())), preferred_element_type=F32)


class Places:
    def __init__(self):
        self.pix, self.pos = lax.axis_index("pix"), lax.axis_index("pos")
        self.z, self.x = self.pos // NX, self.pos % NX

    def at_x(self, d):
        return (self.pix, self.z * NX + (self.x + d) % NX)

    def at_z(self, d):
        return (self.pix, ((self.z + d) % NZ) * NX + self.x)

    def at_pix(self, d):
        return ((self.pix + d) % NP, self.pos)

    def block(self, d):
        return (self.x + d) % NX


def send(src, dst, sems, i, where):
    copy = pltpu.make_async_remote_copy(
        src_ref=src, dst_ref=dst, send_sem=sems.at[0, i], recv_sem=sems.at[1, i],
        device_id=where, device_id_type=MESH,
    )
    copy.start()
    return copy


def rows(start, size):
    return pl.ds(pl.multiple_of(start, size), size)


def sum_and_gather(here, compute, consume, part, held, own, relay, across, zpart, zgot, full, sems):
    copies = []
    part[0] = compute(here.block(2)).astype(BF16)
    low, high = pl.ds(0, HALF), pl.ds(HALF, HALF)
    r0 = send(part.at[0, low], relay.at[0], sems, 0, here.at_x(1))
    r1 = send(part.at[0, high], relay.at[1], sems, 1, here.at_x(3))
    one = compute(here.block(1))
    part[1, HALF:] = one[HALF:].astype(BF16)
    x0 = send(part.at[1, high], across.at[0, high], sems, 2, here.at_x(1))
    held[0] = one[:HALF]
    other = compute(here.block(3))
    part[2, :HALF] = other[:HALF].astype(BF16)
    x1 = send(part.at[2, low], across.at[1, low], sems, 3, here.at_x(3))
    held[1] = other[HALF:]
    own[...] = compute(here.block(0))
    r0.wait_recv()
    part[1, :HALF] = (held[0] + relay[0].astype(F32)).astype(BF16)
    x2 = send(part.at[1, low], across.at[0, low], sems, 4, here.at_x(1))
    r1.wait_recv()
    part[2, HALF:] = (held[1] + relay[1].astype(F32)).astype(BF16)
    x3 = send(part.at[2, high], across.at[1, high], sems, 5, here.at_x(3))
    for c in (x0, x1, x2, x3):
        c.wait_recv()
    own[...] = own[...] + across[0].astype(F32) + across[1].astype(F32)
    zpart[...] = own[...].astype(BF16)
    zs = []
    for i, d in enumerate(FAR_FIRST):
        zs.append(send(zpart.at[rows((here.z + d) % NZ * CHUNK, CHUNK)], zgot.at[i], sems, 6 + i, here.at_z(d)))
    copies += [r0, r1, x0, x1, x2, x3] + zs
    mine = own[rows(here.z * CHUNK, CHUNK), :]
    for i in range(7):
        zs[i].wait_recv()
        mine = mine + zgot[i].astype(F32)
    spot = full.at[rows((here.x * NZ + here.z) * CHUNK, CHUNK)]
    spot[...] = mine.astype(BF16)
    gs = [send(spot, spot, sems, 13 + i, here.at_z(d)) for i, d in enumerate(FAR_FIRST)]
    for c in gs:
        c.wait_recv()

    def half(d, h):
        return full.at[rows(here.block(d) * BLOCK + h * HALF, HALF)]

    a0 = send(half(0, 0), half(0, 0), sems, 20, here.at_x(1))
    b0 = send(half(0, 1), half(0, 1), sems, 21, here.at_x(3))
    b1 = send(half(0, 1), half(0, 1), sems, 22, here.at_x(1))
    a1 = send(half(0, 0), half(0, 0), sems, 23, here.at_x(3))
    consume(here.block(0))
    a0.wait_recv()
    a2 = send(half(3, 0), half(3, 0), sems, 24, here.at_x(1))
    b0.wait_recv()
    b2 = send(half(1, 1), half(1, 1), sems, 25, here.at_x(3))
    b1.wait_recv()
    consume(here.block(3))
    a1.wait_recv()
    consume(here.block(1))
    a2.wait_recv()
    b2.wait_recv()
    consume(here.block(2))
    return copies + gs + [a0, b0, b1, a1, a2, b2]


def sketch_kernel(
    stack, omega, s_out, p_out, g_out,
    m, om, test, part, held, own, relay, across, zpart, zgot, full,
    bt, bparts, bgot, back, grams, total, load_sems, sems, pix_sems,
):
    here = Places()
    barrier = pltpu.get_barrier_semaphore()
    partners = [here.at_x(1), here.at_x(3)]
    partners += [here.at_z(d) for d in FAR_FIRST] + [here.at_pix(d) for d in range(1, NP)]
    for p in partners:
        pl.semaphore_signal(barrier, inc=1, device_id=p, device_id_type=MESH)
    load_om = pltpu.make_async_copy(omega, om, load_sems.at[4])
    load_om.start()
    flat = stack.reshape(ROWS, COLS)
    loads = {}
    for i, d in enumerate((2, 1, 3, 0)):
        where = rows(here.block(d) * BLOCK, BLOCK)
        loads[i] = pltpu.make_async_copy(flat.at[where], m.at[where], load_sems.at[i])
        loads[i].start()
    load_om.wait()
    test[...] = (om[...].astype(F32) / 32768.0).astype(BF16)
    pl.semaphore_wait(barrier, len(partners))

    turn = iter(range(4))

    def first_block(b):
        loads[next(turn)].wait()
        return jnp.dot(m[rows(b * BLOCK, BLOCK), :], test[...], preferred_element_type=F32)

    def take_first(b):
        where = rows(b * BLOCK, BLOCK)
        bt[...] += contract(full[0, where, :], m[where, :], 0, 0)

    bt[...] = jnp.zeros_like(bt)
    copies = sum_and_gather(
        here, first_block, take_first, part.at[0], held.at[0], own, relay.at[0],
        across.at[0], zpart.at[0], zgot.at[0], full.at[0], sems.at[0],
    )

    for j in range(NP):
        bparts[j] = bt[:, j * K:(j + 1) * K].astype(BF16)
        total[j] = bt[:, j * K:(j + 1) * K]
    bs = []
    for d in range(1, NP):
        bs.append(send(bparts.at[(here.pix + d) % NP], bgot.at[d - 1], pix_sems.at[0], d - 1, here.at_pix(d)))
    mine = total[here.pix]
    for d in range(1, NP):
        bs[d - 1].wait_recv()
        mine = mine + bgot[d - 1].astype(F32)
    spot = back.at[rows(here.pix * K, K)]
    spot[...] = mine.T.astype(BF16)
    gs = [send(spot, spot, pix_sems.at[1], d - 1, here.at_pix(d)) for d in range(1, NP)]
    for c in gs:
        c.wait_recv()
    copies += bs + gs

    def sketch_block(b):
        return jnp.dot(m[rows(b * BLOCK, BLOCK), :], back[...], preferred_element_type=F32)

    def take_sketch(b):
        where = rows(b * BLOCK, BLOCK)
        s = full[1, where, :]
        total[b] = contract(s, s, 0, 0)
        p_out[...] += contract(s, m[where, :], 0, 0)

    p_out[...] = jnp.zeros_like(p_out)
    copies += sum_and_gather(
        here, sketch_block, take_sketch, part.at[1], held.at[1], own, relay.at[1],
        across.at[1], zpart.at[1], zgot.at[1], full.at[1], sems.at[1],
    )
    grams[here.pix] = total[0] + total[1] + total[2] + total[3]
    mine = grams.at[here.pix]
    gs = [send(mine, mine, pix_sems.at[2], d - 1, here.at_pix(d)) for d in range(1, NP)]
    s_out[...] = full[1]
    for c in gs:
        c.wait_recv()
    gram = grams[0]
    for j in range(1, NP):
        gram = gram + grams[j]
    g_out[...] = gram
    for c in copies + gs:
        c.wait_send()


def sketch_call(stack, omega):
    vmem = pl.BlockSpec(memory_space=pltpu.VMEM)
    hbm = pl.BlockSpec(memory_space=pl.ANY)
    return pl.pallas_call(
        sketch_kernel,
        out_shape=(
            jax.ShapeDtypeStruct((ROWS, K), BF16),
            jax.ShapeDtypeStruct((K, COLS), F32),
            jax.ShapeDtypeStruct((K, K), F32),
        ),
        in_specs=[hbm, hbm],
        out_specs=(vmem, vmem, vmem),
        scratch_shapes=[
            pltpu.VMEM((ROWS, COLS), BF16),
            pltpu.VMEM((COLS, K), jnp.int32),
            pltpu.VMEM((COLS, K), BF16),
            pltpu.VMEM((2, 3, BLOCK, K), BF16),
            pltpu.VMEM((2, 2, HALF, K), F32),
            pltpu.VMEM((BLOCK, K), F32),
            pltpu.VMEM((2, 2, HALF, K), BF16),
            pltpu.VMEM((2, 2, BLOCK, K), BF16),
            pltpu.VMEM((2, BLOCK, K), BF16),
            pltpu.VMEM((2, 7, CHUNK, K), BF16),
            pltpu.VMEM((2, ROWS, K), BF16),
            pltpu.VMEM((K, COLS), F32),
            pltpu.VMEM((NP, K, K), BF16),
            pltpu.VMEM((NP - 1, K, K), BF16),
            pltpu.VMEM((COLS, K), BF16),
            pltpu.VMEM((NP, K, K), F32),
            pltpu.VMEM((NP, K, K), F32),
            pltpu.SemaphoreType.DMA((5,)),
            pltpu.SemaphoreType.DMA((2, 2, 26)),
            pltpu.SemaphoreType.DMA((3, 2, NP - 1)),
        ],
        compiler_params=pltpu.CompilerParams(
            collective_id=0, has_side_effects=True, vmem_limit_bytes=48 << 20
        ),
        cost_estimate=pl.CostEstimate(flops=4 * 2 * ROWS * COLS * K, bytes_accessed=12 << 20, transcendentals=0),
    )(stack, omega)


def project_kernel(p_ref, inv_ref, o_ref, parts, got, sems):
    here = Places()
    barrier = pltpu.get_barrier_semaphore()
    for d in range(1, NP):
        pl.semaphore_signal(barrier, inc=1, device_id=here.at_pix(d), device_id_type=MESH)
    mine = lax.dot_general(
        inv_ref[...], p_ref[...], (((1,), (0,)), ((), ())),
        precision=lax.Precision.HIGHEST, preferred_element_type=F32,
    )
    parts[...] = mine.reshape(NP, K // NP, COLS)
    pl.semaphore_wait(barrier, NP - 1)
    copies = []
    for d in range(1, NP):
        copies.append(send(parts.at[(here.pix + d) % NP], got.at[d - 1], sems, d - 1, here.at_pix(d)))
    total = parts[here.pix]
    for d in range(1, NP):
        copies[d - 1].wait_recv()
        total = total + got[d - 1]
    o_ref[...] = total
    for c in copies:
        c.wait_send()


def project_call(p, inverse):
    vmem = pl.BlockSpec(memory_space=pltpu.VMEM)
    return pl.pallas_call(
        project_kernel,
        out_shape=jax.ShapeDtypeStruct((K // NP, COLS), F32),
        in_specs=[vmem, vmem],
        out_specs=vmem,
        scratch_shapes=[
            pltpu.VMEM((NP, K // NP, COLS), F32),
            pltpu.VMEM((NP - 1, K // NP, COLS), F32),
            pltpu.SemaphoreType.DMA((2, NP - 1)),
        ],
        compiler_params=pltpu.CompilerParams(
            collective_id=1, has_side_effects=True, vmem_limit_bytes=16 << 20
        ),
    )(p, inverse)


def body(stack, omega):
    sketch, p, gram = sketch_call(stack, omega)
    lower = jnp.linalg.cholesky(gram)
    inverse = lax.linalg.triangular_solve(
        lower, jnp.eye(K, dtype=F32), left_side=True, lower=True
    )
    projected = project_call(p, inverse)
    scale_factor = math.sqrt(2.0 * stack.shape[0] * lax.axis_size("pix"))
    q_full = jnp.dot(
        sketch.astype(F32), inverse.T, precision=lax.Precision.HIGHEST, preferred_element_type=F32
    )
    basis = (q_full * scale_factor).reshape(stack.shape[0], 2, K)
    return (basis, projected)


def solution(mesh):
    return jax.shard_map(
        body,
        mesh=mesh,
        in_specs=(P("pix", None, "pos"), P("pos", None)),
        out_specs=(P("pix", None, None), P("pix", "pos")),
        check_vma=False,
    )
```

```python
import math

import jax
import jax.numpy as jnp
from jax import lax
from jax.experimental import pallas as pl
from jax.experimental.pallas import tpu as pltpu
from jax.sharding import PartitionSpec as P

MESH = pl.DeviceIdType.MESH
K = 128
NX = 4
NZ = 8
NP = 8
ROWS = 4096
COLS = 1024
BLOCK = ROWS // NX
CHUNK = BLOCK // NZ
FAR_FIRST = (4, 3, 5, 2, 6, 1, 7, 0)
NEAR_FIRST = (0, 1, 7, 2, 6, 3, 5, 4)
LAG = 2
PANEL = 32
HALF_K = K // 2
SCALE = math.sqrt(float(ROWS * NP))
F32 = jnp.float32
BF16 = jnp.bfloat16


def contract(left, right, a, b):
    return lax.dot_general(left, right, (((a,), (b,)), ((), ())), preferred_element_type=F32)


class Places:
    def __init__(self):
        self.pix, self.pos = lax.axis_index("pix"), lax.axis_index("pos")
        self.z, self.x = self.pos // NX, self.pos % NX

    def at_x(self, d):
        return (self.pix, self.z * NX + (self.x + d) % NX)

    def at_z(self, d):
        return (self.pix, ((self.z + d) % NZ) * NX + self.x)

    def at_pix(self, d):
        return ((self.pix + d) % NP, self.pos)

    def block(self, d):
        return (self.x + d) % NX


def send(src, dst, sems, i, where):
    copy = pltpu.make_async_remote_copy(
        src_ref=src, dst_ref=dst, send_sem=sems.at[0, i], recv_sem=sems.at[1, i],
        device_id=where, device_id_type=MESH,
    )
    copy.start()
    return copy


def rows(start, size):
    return pl.ds(pl.multiple_of(start, size), size)


def sum_and_gather(here, compute, consume, part, held, own, relay, across, zpart, zgot, full, sems):
    done = []

    def chunk(i):
        return rows((here.z + FAR_FIRST[i]) % NZ * CHUNK, CHUNK)

    part[0] = compute(here.block(2)).astype(BF16)
    relays = []
    for i in range(NZ):
        relays.append(send(part.at[0, chunk(i)], relay.at[i], sems, i, here.at_x(1 if i % 2 == 0 else 3)))
    plus, minus = {}, {}
    held[0] = compute(here.block(1))
    part[1] = held[0].astype(BF16)
    for i in range(1, NZ, 2):
        plus[i] = send(part.at[1, chunk(i)], across.at[0, i], sems, NZ + i, here.at_x(1))
    held[1] = compute(here.block(3))
    part[2] = held[1].astype(BF16)
    for i in range(0, NZ, 2):
        minus[i] = send(part.at[2, chunk(i)], across.at[1, i], sems, 2 * NZ + i, here.at_x(3))
    own[...] = compute(here.block(0))
    zs = []
    mine = None
    for step in range(NZ + LAG):
        if step < NZ:
            i = step
            relays[i].wait_recv()
            if i % 2 == 0:
                part[1, chunk(i)] = (held[0, chunk(i)] + relay[i].astype(F32)).astype(BF16)
                plus[i] = send(part.at[1, chunk(i)], across.at[0, i], sems, NZ + i, here.at_x(1))
            else:
                part[2, chunk(i)] = (held[1, chunk(i)] + relay[i].astype(F32)).astype(BF16)
                minus[i] = send(part.at[2, chunk(i)], across.at[1, i], sems, 2 * NZ + i, here.at_x(3))
        if step >= LAG:
            i = step - LAG
            plus[i].wait_recv()
            minus[i].wait_recv()
            mine = own[chunk(i), :] + across[0, i].astype(F32) + across[1, i].astype(F32)
            if i < NZ - 1:
                zpart[i] = mine.astype(BF16)
                zs.append(send(zpart.at[i], zgot.at[i], sems, 3 * NZ + i, here.at_z(FAR_FIRST[i])))
    for i in range(NZ - 1):
        zs[i].wait_recv()
        mine = mine + zgot[i].astype(F32)
    done += relays + list(plus.values()) + list(minus.values()) + zs

    def place(dx, dz):
        return full.at[rows((here.block(dx) * NZ + (here.z + dz) % NZ) * CHUNK, CHUNK)]

    spot = place(0, 0)
    spot[...] = mine.astype(BF16)
    gs = {}
    for d in NEAR_FIRST[1:]:
        gs[d] = send(spot, spot, sems, 4 * NZ + d, here.at_z(d))
    plus, minus, forward = [], [], []
    for step in range(NZ + LAG):
        if step < NZ:
            d = NEAR_FIRST[step]
            if d:
                gs[NZ - d].wait_recv()
            spot = place(0, d)
            plus.append(send(spot, spot, sems, 5 * NZ + step, here.at_x(1)))
            minus.append(send(spot, spot, sems, 6 * NZ + step, here.at_x(3)))
        if step == NZ - 1:
            consume(here.block(0))
        if step >= LAG:
            i = step - LAG
            d = NEAR_FIRST[i]
            if i % 2 == 0:
                plus[i].wait_recv()
                spot, to = place(3, d), here.at_x(1)
            else:
                minus[i].wait_recv()
                spot, to = place(1, d), here.at_x(3)
            forward.append(send(spot, spot, sems, 7 * NZ + i, to))
    for i in range(1, NZ, 2):
        plus[i].wait_recv()
    consume(here.block(3))
    for i in range(0, NZ, 2):
        minus[i].wait_recv()
    consume(here.block(1))
    for i in range(NZ):
        forward[i].wait_recv()
    consume(here.block(2))
    return done + list(gs.values()) + plus + minus + forward


def inverse_factor(gram):
    ids = lax.broadcasted_iota(jnp.int32, (K, K), 0)
    a, v = gram, (ids == lax.broadcasted_iota(jnp.int32, (K, K), 1)).astype(F32)
    row = lax.broadcasted_iota(jnp.int32, (PANEL, K), 0)
    out = []
    for lo in range(0, K, PANEL):
        ap, vp = a[:PANEL], v[:PANEL]
        c = jnp.stack([jnp.broadcast_to(ap[:, lo + k:lo + k + 1], (PANEL, K)) for k in range(PANEL)])
        for j in range(PANEL):
            r = lax.rsqrt(jnp.broadcast_to(c[0, j:j + 1], (PANEL, K)))
            below = jnp.where(row > j, c[0] * r, 0.0)
            ra, rv = ap[j:j + 1] * r, vp[j:j + 1] * r
            ap = jnp.where(row == j, ra, ap - below * ra)
            vp = jnp.where(row == j, rv, vp - below * rv)
            if j + 1 < PANEL:
                c = c[1:]
                c = c - below[None] * (c[:, j:j + 1, :] * r[None])
        out.append(vp)
        if lo + PANEL < K:
            both = lax.dot_general(
                ap, jnp.concatenate([ap, vp], axis=1), (((0,), (0,)), ((), ())),
                precision=lax.Precision.HIGHEST, preferred_element_type=F32,
            )
            a = a[PANEL:] - both[lo + PANEL:, :K]
            v = v[PANEL:] - both[lo + PANEL:, K:]
    return jnp.concatenate(out, axis=0)


def whole_kernel(
    stack, omega, basis_out, projected_out,
    m, om, test, part, held, own, relay, across, zpart, zgot, full,
    bt, bparts, bgot, back, total, mine_gram, half_got, halves, gram, pparts, pgot,
    load_sems, sems, pix_sems, gram_sems,
):
    here = Places()
    barrier = pltpu.get_barrier_semaphore()
    partners = [here.at_x(1), here.at_x(3)]
    partners += [here.at_z(d) for d in range(1, NZ)] + [here.at_pix(d) for d in range(1, NP)]
    for p in partners:
        pl.semaphore_signal(barrier, inc=1, device_id=p, device_id_type=MESH)
    load_om = pltpu.make_async_copy(omega, om, load_sems.at[4])
    load_om.start()
    flat = stack.reshape(ROWS, COLS)
    loads = []
    for i, d in enumerate((2, 1, 3, 0)):
        where = rows(here.block(d) * BLOCK, BLOCK)
        loads.append(pltpu.make_async_copy(flat.at[where], m.at[where], load_sems.at[i]))
        loads[i].start()
    load_om.wait()
    test[...] = (om[...].astype(F32) / 32768.0).astype(BF16)
    pl.semaphore_wait(barrier, len(partners))

    turn = iter(loads)

    def first_block(b):
        next(turn).wait()
        return jnp.dot(m[rows(b * BLOCK, BLOCK), :], test[...], preferred_element_type=F32)

    def take_first(b):
        where = rows(b * BLOCK, BLOCK)
        bt[...] += contract(full[0, where, :], m[where, :], 0, 0)

    bt[...] = jnp.zeros_like(bt)
    copies = sum_and_gather(
        here, first_block, take_first, part.at[0], held, own, relay.at[0],
        across.at[0], zpart.at[0], zgot.at[0], full.at[0], sems.at[0],
    )

    for j in range(NP):
        bparts[j] = bt[:, j * K:(j + 1) * K].astype(BF16)
        total[j] = bt[:, j * K:(j + 1) * K]
    bs = []
    for d in range(1, NP):
        bs.append(send(bparts.at[(here.pix + d) % NP], bgot.at[d - 1], pix_sems.at[0], d - 1, here.at_pix(d)))
    mine = total[here.pix]
    for d in range(1, NP):
        bs[d - 1].wait_recv()
        mine = mine + bgot[d - 1].astype(F32)
    spot = back.at[rows(here.pix * K, K)]
    spot[...] = mine.T.astype(BF16)
    gs = [send(spot, spot, pix_sems.at[1], d - 1, here.at_pix(d)) for d in range(1, NP)]
    for c in gs:
        c.wait_recv()
    copies += bs + gs

    def sketch_block(b):
        return jnp.dot(m[rows(b * BLOCK, BLOCK), :], back[...], preferred_element_type=F32)

    def take_sketch(b):
        where = rows(b * BLOCK, BLOCK)
        s = full[1, where, :]
        total[b] = contract(s, s, 0, 0)
        bt[...] += contract(s, m[where, :], 0, 0)

    bt[...] = jnp.zeros_like(bt)
    copies += sum_and_gather(
        here, sketch_block, take_sketch, part.at[1], held, own, relay.at[1],
        across.at[1], zpart.at[1], zgot.at[1], full.at[1], sems.at[1],
    )

    y, core = here.pix // 2, here.pix % 2
    near = (y * 2 + 1 - core, here.pos)
    mine_gram[...] = total[0] + total[1] + total[2] + total[3]
    keep, give = rows(core * HALF_K, HALF_K), rows((1 - core) * HALF_K, HALF_K)
    swap = send(mine_gram.at[give], half_got, gram_sems, 0, near)
    swap.wait_recv()
    halves[y] = mine_gram[keep, :] + half_got[...]
    spot = halves.at[y]
    ys = [send(spot, spot, gram_sems, d, ((y + d) % 4 * 2 + core, here.pos)) for d in (1, 2, 3)]
    for c in ys:
        c.wait_recv()
    gram[keep, :] = (halves[0] + halves[1]) + (halves[2] + halves[3])
    spot = gram.at[keep]
    swap_back = send(spot, spot, gram_sems, 4, near)
    swap_back.wait_recv()
    copies += [swap, swap_back] + ys
    inverse = inverse_factor(gram[...])

    product = lax.dot_general(
        inverse, bt[...], (((1,), (0,)), ((), ())),
        precision=lax.Precision.HIGHEST, preferred_element_type=F32,
    )
    bt[...] = product
    pparts[...] = product.astype(BF16)
    share = K // NP
    ps = []
    for d in range(1, NP):
        to = (here.pix + d) % NP
        ps.append(send(pparts.at[rows(to * share, share)], pgot.at[d - 1], pix_sems.at[2], d - 1, here.at_pix(d)))

    scaled = inverse.T * SCALE
    top = scaled.astype(BF16)
    rest = scaled - top.astype(F32)
    mid = rest.astype(BF16)
    low = (rest - mid.astype(F32)).astype(BF16)
    for b in range(NX):
        where = pl.ds(b * BLOCK, BLOCK)
        s = full[1, where, :]
        basis_out[where, :] = (
            jnp.dot(s, top, preferred_element_type=F32)
            + jnp.dot(s, mid, preferred_element_type=F32)
            + jnp.dot(s, low, preferred_element_type=F32)
        )
    mine = bt[rows(here.pix * share, share), :]
    for d in range(1, NP):
        ps[d - 1].wait_recv()
        mine = mine + pgot[d - 1].astype(F32)
    projected_out[...] = mine
    for c in copies + ps:
        c.wait_send()


def body(stack, omega):
    vmem = pl.BlockSpec(memory_space=pltpu.VMEM)
    hbm = pl.BlockSpec(memory_space=pl.ANY)
    basis, projected = pl.pallas_call(
        whole_kernel,
        out_shape=(
            jax.ShapeDtypeStruct((ROWS, K), F32),
            jax.ShapeDtypeStruct((K // NP, COLS), F32),
        ),
        in_specs=[hbm, hbm],
        out_specs=(vmem, vmem),
        scratch_shapes=[
            pltpu.VMEM((ROWS, COLS), BF16),
            pltpu.VMEM((COLS, K), jnp.int32),
            pltpu.VMEM((COLS, K), BF16),
            pltpu.VMEM((2, 3, BLOCK, K), BF16),
            pltpu.VMEM((2, BLOCK, K), F32),
            pltpu.VMEM((BLOCK, K), F32),
            pltpu.VMEM((2, NZ, CHUNK, K), BF16),
            pltpu.VMEM((2, 2, NZ, CHUNK, K), BF16),
            pltpu.VMEM((2, NZ - 1, CHUNK, K), BF16),
            pltpu.VMEM((2, NZ - 1, CHUNK, K), BF16),
            pltpu.VMEM((2, ROWS, K), BF16),
            pltpu.VMEM((K, COLS), F32),
            pltpu.VMEM((NP, K, K), BF16),
            pltpu.VMEM((NP - 1, K, K), BF16),
            pltpu.VMEM((COLS, K), BF16),
            pltpu.VMEM((NP, K, K), F32),
            pltpu.VMEM((K, K), F32),
            pltpu.VMEM((HALF_K, K), F32),
            pltpu.VMEM((4, HALF_K, K), F32),
            pltpu.VMEM((K, K), F32),
            pltpu.VMEM((K, COLS), BF16),
            pltpu.VMEM((NP - 1, K // NP, COLS), BF16),
            pltpu.SemaphoreType.DMA((5,)),
            pltpu.SemaphoreType.DMA((2, 2, 8 * NZ)),
            pltpu.SemaphoreType.DMA((3, 2, NP - 1)),
            pltpu.SemaphoreType.DMA((2, 5)),
        ],
        compiler_params=pltpu.CompilerParams(
            collective_id=0, has_side_effects=True, vmem_limit_bytes=48 << 20
        ),
        cost_estimate=pl.CostEstimate(flops=4 * 2 * ROWS * COLS * K, bytes_accessed=12 << 20, transcendentals=0),
    )(stack, omega)
    return basis.reshape(stack.shape[0], 2, K), projected


def solution(mesh):
    return jax.shard_map(
        body,
        mesh=mesh,
        in_specs=(P("pix", None, "pos"), P("pos", None)),
        out_specs=(P("pix", None, None), P("pix", "pos")),
        check_vma=False,
    )
```

```python
import math

import jax
import jax.numpy as jnp
from jax import lax
from jax.experimental import pallas as pl
from jax.experimental.pallas import tpu as pltpu
from jax.sharding import PartitionSpec as P

MESH = pl.DeviceIdType.MESH
K = 128
NX = 4
NZ = 8
NP = 8
ROWS = 4096
COLS = 1024
BLOCK = ROWS // NX
CHUNK = BLOCK // NZ
FAR_FIRST = (4, 3, 5, 2, 6, 1, 7, 0)
NEAR_FIRST = (0, 1, 7, 2, 6, 3, 5, 4)
LAG = 2
RELAYED = (4, 5, 6, 7)
FORWARDED = (0, 1)
PANEL = 32
HALF_K = K // 2
SCALE = math.sqrt(float(ROWS * NP))
F32 = jnp.float32
BF16 = jnp.bfloat16


def contract(left, right, a, b):
    return lax.dot_general(left, right, (((a,), (b,)), ((), ())), preferred_element_type=F32)


class Places:
    def __init__(self):
        self.pix, self.pos = lax.axis_index("pix"), lax.axis_index("pos")
        self.z, self.x = self.pos // NX, self.pos % NX

    def at_x(self, d):
        return (self.pix, self.z * NX + (self.x + d) % NX)

    def at_z(self, d):
        return (self.pix, ((self.z + d) % NZ) * NX + self.x)

    def at_pix(self, d):
        return ((self.pix + d) % NP, self.pos)

    def block(self, d):
        return (self.x + d) % NX


def send(src, dst, sems, i, where):
    copy = pltpu.make_async_remote_copy(
        src_ref=src, dst_ref=dst, send_sem=sems.at[0, i], recv_sem=sems.at[1, i],
        device_id=where, device_id_type=MESH,
    )
    copy.start()
    return copy


def rows(start, size):
    return pl.ds(pl.multiple_of(start, size), size)


def sum_and_gather(here, compute, consume, part, held, own, relay, across, zpart, zgot, full, sems, enter=None):
    done = []

    def chunk(i):
        return rows((here.z + FAR_FIRST[i]) % NZ * CHUNK, CHUNK)

    part[0] = compute(here.block(2)).astype(BF16)
    if enter is not None:
        enter()
    relays = []
    for i in range(NZ):
        if i in RELAYED:
            relays.append(send(part.at[0, chunk(i)], relay.at[i], sems, i, here.at_x(1 if i % 2 == 0 else 3)))
        else:
            relays.append(send(part.at[0, chunk(i)], across.at[2, i], sems, i, here.at_x(2)))
    held[0] = compute(here.block(1))
    part[1] = held[0].astype(BF16)
    held[1] = compute(here.block(3))
    part[2] = held[1].astype(BF16)
    own[...] = compute(here.block(0))
    plus, minus = {}, {}
    for i in range(NZ):
        if i % 2 == 1 or i not in RELAYED:
            plus[i] = send(part.at[1, chunk(i)], across.at[0, i], sems, NZ + i, here.at_x(1))
        if i % 2 == 0 or i not in RELAYED:
            minus[i] = send(part.at[2, chunk(i)], across.at[1, i], sems, 2 * NZ + i, here.at_x(3))
    zs = []
    mine = None
    for step in range(NZ + LAG):
        if step < NZ:
            i = step
            if i in RELAYED:
                relays[i].wait_recv()
            if i in RELAYED and i % 2 == 0:
                part[1, chunk(i)] = (held[0, chunk(i)] + relay[i].astype(F32)).astype(BF16)
                plus[i] = send(part.at[1, chunk(i)], across.at[0, i], sems, NZ + i, here.at_x(1))
            elif i in RELAYED:
                part[2, chunk(i)] = (held[1, chunk(i)] + relay[i].astype(F32)).astype(BF16)
                minus[i] = send(part.at[2, chunk(i)], across.at[1, i], sems, 2 * NZ + i, here.at_x(3))
        if step >= LAG:
            i = step - LAG
            plus[i].wait_recv()
            minus[i].wait_recv()
            mine = own[chunk(i), :] + across[0, i].astype(F32) + across[1, i].astype(F32)
            if i not in RELAYED:
                relays[i].wait_recv()
                mine = mine + across[2, i].astype(F32)
            if i < NZ - 1:
                zpart[i] = mine.astype(BF16)
                zs.append(send(zpart.at[i], zgot.at[i], sems, 3 * NZ + i, here.at_z(FAR_FIRST[i])))
    for i in range(NZ - 1):
        zs[i].wait_recv()
        mine = mine + zgot[i].astype(F32)
    done += relays + list(plus.values()) + list(minus.values()) + zs

    def place(dx, dz):
        return full.at[rows((here.block(dx) * NZ + (here.z + dz) % NZ) * CHUNK, CHUNK)]

    spot = place(0, 0)
    spot[...] = mine.astype(BF16)
    gs = {}
    for d in NEAR_FIRST[1:]:
        gs[d] = send(spot, spot, sems, 4 * NZ + d, here.at_z(d))
    plus, minus, forward = [], [], {}
    for step in range(NZ + LAG):
        if step < NZ:
            d = NEAR_FIRST[step]
            if d:
                gs[NZ - d].wait_recv()
            spot = place(0, d)
            plus.append(send(spot, spot, sems, 5 * NZ + step, here.at_x(1)))
            minus.append(send(spot, spot, sems, 6 * NZ + step, here.at_x(3)))
            if step not in FORWARDED:
                forward[step] = send(spot, spot, sems, 7 * NZ + step, here.at_x(2))
        if step == NZ - 1:
            consume(here.block(0))
        if step >= LAG:
            i = step - LAG
            d = NEAR_FIRST[i]
            if i not in FORWARDED:
                continue
            if i % 2 == 0:
                plus[i].wait_recv()
                spot, to = place(3, d), here.at_x(1)
            else:
                minus[i].wait_recv()
                spot, to = place(1, d), here.at_x(3)
            forward[i] = send(spot, spot, sems, 7 * NZ + i, to)
    for i in range(NZ):
        if i % 2 == 1 or i not in FORWARDED:
            plus[i].wait_recv()
    consume(here.block(3))
    for i in range(NZ):
        if i % 2 == 0 or i not in FORWARDED:
            minus[i].wait_recv()
    consume(here.block(1))
    for i in range(NZ):
        forward[i].wait_recv()
    consume(here.block(2))
    return done + list(gs.values()) + plus + minus + list(forward.values())


def inverse_factor(gram):
    ids = lax.broadcasted_iota(jnp.int32, (K, K), 0)
    a, v = gram, (ids == lax.broadcasted_iota(jnp.int32, (K, K), 1)).astype(F32)
    row = lax.broadcasted_iota(jnp.int32, (PANEL, K), 0)
    out = []
    for lo in range(0, K, PANEL):
        ap, vp = a[:PANEL], v[:PANEL]
        c = jnp.stack([jnp.broadcast_to(ap[:, lo + k:lo + k + 1], (PANEL, K)) for k in range(PANEL)])
        for j in range(PANEL):
            r = lax.rsqrt(jnp.broadcast_to(c[0, j:j + 1], (PANEL, K)))
            below = jnp.where(row > j, c[0] * r, 0.0)
            ra, rv = ap[j:j + 1] * r, vp[j:j + 1] * r
            ap = jnp.where(row == j, ra, ap - below * ra)
            vp = jnp.where(row == j, rv, vp - below * rv)
            if j + 1 < PANEL:
                c = c[1:]
                c = c - below[None] * (c[:, j:j + 1, :] * r[None])
        out.append(vp)
        if lo + PANEL < K:
            both = lax.dot_general(
                ap, jnp.concatenate([ap, vp], axis=1), (((0,), (0,)), ((), ())),
                precision=lax.Precision.HIGHEST, preferred_element_type=F32,
            )
            a = a[PANEL:] - both[lo + PANEL:, :K]
            v = v[PANEL:] - both[lo + PANEL:, K:]
    return jnp.concatenate(out, axis=0)


def thirds(value):
    top = value.astype(BF16)
    rest = value - top.astype(F32)
    mid = rest.astype(BF16)
    return top, mid, (rest - mid.astype(F32)).astype(BF16)


def whole_kernel(
    stack, omega, basis_out, projected_out,
    m, om, test, part, held, own, relay, across, zpart, zgot, full,
    bt, bparts, bgot, back, total, mine_gram, half_got, halves, gram, factor, pparts, pgot, pall,
    load_sems, sems, pix_sems, gram_sems,
):
    here = Places()
    barrier = pltpu.get_barrier_semaphore()
    partners = [here.at_x(d) for d in range(1, NX)]
    partners += [here.at_z(d) for d in range(1, NZ)] + [here.at_pix(d) for d in range(1, NP)]
    for p in partners:
        pl.semaphore_signal(barrier, inc=1, device_id=p, device_id_type=MESH)
    load_om = pltpu.make_async_copy(omega, om, load_sems.at[4])
    load_om.start()
    flat = stack.reshape(ROWS, COLS)
    loads = []
    for i, d in enumerate((2, 1, 3, 0)):
        where = rows(here.block(d) * BLOCK, BLOCK)
        loads.append(pltpu.make_async_copy(flat.at[where], m.at[where], load_sems.at[i]))
        loads[i].start()
    load_om.wait()
    test[...] = (om[...].astype(F32) / 32768.0).astype(BF16)
    turn = iter(loads)

    def first_block(b):
        next(turn).wait()
        return jnp.dot(m[rows(b * BLOCK, BLOCK), :], test[...], preferred_element_type=F32)

    def take_first(b):
        where = rows(b * BLOCK, BLOCK)
        bt[...] += contract(full[0, where, :], m[where, :], 0, 0)

    bt[...] = jnp.zeros_like(bt)
    copies = sum_and_gather(
        here, first_block, take_first, part.at[0], held, own, relay.at[0],
        across.at[0], zpart.at[0], zgot.at[0], full.at[0], sems.at[0],
        lambda: pl.semaphore_wait(barrier, len(partners)),
    )

    for j in range(NP):
        bparts[j] = bt[:, j * K:(j + 1) * K].astype(BF16)
        total[j] = bt[:, j * K:(j + 1) * K]
    bs = []
    for d in range(1, NP):
        bs.append(send(bparts.at[(here.pix + d) % NP], bgot.at[d - 1], pix_sems.at[0], d - 1, here.at_pix(d)))
    mine = total[here.pix]
    for d in range(1, NP):
        bs[d - 1].wait_recv()
        mine = mine + bgot[d - 1].astype(F32)
    spot = back.at[rows(here.pix * K, K)]
    spot[...] = mine.T.astype(BF16)
    gs = [send(spot, spot, pix_sems.at[1], d - 1, here.at_pix(d)) for d in range(1, NP)]
    for c in gs:
        c.wait_recv()
    copies += bs + gs

    def sketch_block(b):
        return jnp.dot(m[rows(b * BLOCK, BLOCK), :], back[...], preferred_element_type=F32)

    def take_sketch(b):
        where = rows(b * BLOCK, BLOCK)
        s = full[1, where, :]
        total[b] = contract(s, s, 0, 0)
        bt[...] += contract(s, m[where, :], 0, 0)

    bt[...] = jnp.zeros_like(bt)
    copies += sum_and_gather(
        here, sketch_block, take_sketch, part.at[1], held, own, relay.at[1],
        across.at[1], zpart.at[1], zgot.at[1], full.at[1], sems.at[1],
    )

    y, core = here.pix // 2, here.pix % 2
    near = (y * 2 + 1 - core, here.pos)
    mine_gram[...] = total[0] + total[1] + total[2] + total[3]
    keep, give = rows(core * HALF_K, HALF_K), rows((1 - core) * HALF_K, HALF_K)
    swap = send(mine_gram.at[give], half_got, gram_sems, 0, near)
    swap.wait_recv()
    halves[y] = mine_gram[keep, :] + half_got[...]
    spot = halves.at[y]
    ys = [send(spot, spot, gram_sems, d, ((y + d) % 4 * 2 + core, here.pos)) for d in (1, 2, 3)]
    for j in range(NP):
        pparts[j] = bt[:, j * K:(j + 1) * K].astype(BF16)
        total[j] = bt[:, j * K:(j + 1) * K]
    ps = []
    for d in range(1, NP):
        ps.append(send(pparts.at[(here.pix + d) % NP], pgot.at[d - 1], pix_sems.at[2], d - 1, here.at_pix(d)))
    for c in ys:
        c.wait_recv()
    gram[keep, :] = (halves[0] + halves[1]) + (halves[2] + halves[3])
    spot = gram.at[keep]
    swap_back = send(spot, spot, gram_sems, 4, near)
    mine = total[here.pix]
    for d in range(1, NP):
        ps[d - 1].wait_recv()
        mine = mine + pgot[d - 1].astype(F32)
    pall[here.pix] = mine.astype(BF16)
    spot = pall.at[here.pix]
    gs = [send(spot, spot, pix_sems.at[3], d - 1, here.at_pix(d)) for d in range(1, NP)]
    swap_back.wait_recv()
    copies += [swap, swap_back] + ys + ps + gs
    inverse = inverse_factor(gram[...])
    factor[...] = inverse

    scaled = inverse.T * SCALE
    top, mid, low = thirds(scaled)
    for b in range(NX):
        where = pl.ds(b * BLOCK, BLOCK)
        s = full[1, where, :]
        basis_out[where, :] = (
            jnp.dot(s, top, preferred_element_type=F32)
            + jnp.dot(s, mid, preferred_element_type=F32)
            + jnp.dot(s, low, preferred_element_type=F32)
        )
    share = K // NP
    lines = jnp.concatenate(thirds(factor[rows(here.pix * share, share), :]), axis=0)
    for c in gs:
        c.wait_recv()
    for j in range(NP):
        product = jnp.dot(lines, pall[j], preferred_element_type=F32)
        projected_out[:, j * K:(j + 1) * K] = product[:share] + product[share:2 * share] + product[2 * share:]
    for c in copies:
        c.wait_send()


def body(stack, omega):
    vmem = pl.BlockSpec(memory_space=pltpu.VMEM)
    hbm = pl.BlockSpec(memory_space=pl.ANY)
    basis, projected = pl.pallas_call(
        whole_kernel,
        out_shape=(
            jax.ShapeDtypeStruct((ROWS, K), F32),
            jax.ShapeDtypeStruct((K // NP, COLS), F32),
        ),
        in_specs=[hbm, pl.BlockSpec(memory_space=pltpu.HBM)],
        out_specs=(vmem, vmem),
        scratch_shapes=[
            pltpu.VMEM((ROWS, COLS), BF16),
            pltpu.VMEM((COLS, K), jnp.int32),
            pltpu.VMEM((COLS, K), BF16),
            pltpu.VMEM((2, 3, BLOCK, K), BF16),
            pltpu.VMEM((2, BLOCK, K), F32),
            pltpu.VMEM((BLOCK, K), F32),
            pltpu.VMEM((2, NZ, CHUNK, K), BF16),
            pltpu.VMEM((2, 3, NZ, CHUNK, K), BF16),
            pltpu.VMEM((2, NZ - 1, CHUNK, K), BF16),
            pltpu.VMEM((2, NZ - 1, CHUNK, K), BF16),
            pltpu.VMEM((2, ROWS, K), BF16),
            pltpu.VMEM((K, COLS), F32),
            pltpu.VMEM((NP, K, K), BF16),
            pltpu.VMEM((NP - 1, K, K), BF16),
            pltpu.VMEM((COLS, K), BF16),
            pltpu.VMEM((NP, K, K), F32),
            pltpu.VMEM((K, K), F32),
            pltpu.VMEM((HALF_K, K), F32),
            pltpu.VMEM((4, HALF_K, K), F32),
            pltpu.VMEM((K, K), F32),
            pltpu.VMEM((K, K), F32),
            pltpu.VMEM((NP, K, K), BF16),
            pltpu.VMEM((NP - 1, K, K), BF16),
            pltpu.VMEM((NP, K, K), BF16),
            pltpu.SemaphoreType.DMA((5,)),
            pltpu.SemaphoreType.DMA((2, 2, 8 * NZ)),
            pltpu.SemaphoreType.DMA((4, 2, NP - 1)),
            pltpu.SemaphoreType.DMA((2, 5)),
        ],
        compiler_params=pltpu.CompilerParams(
            collective_id=0, has_side_effects=True, vmem_limit_bytes=48 << 20
        ),
        cost_estimate=pl.CostEstimate(flops=4 * 2 * ROWS * COLS * K, bytes_accessed=12 << 20, transcendentals=0),
    )(stack, omega)
    return basis.reshape(stack.shape[0], 2, K), projected


def solution(mesh):
    return jax.shard_map(
        body,
        mesh=mesh,
        in_specs=(P("pix", None, "pos"), P("pos", None)),
        out_specs=(P("pix", None, None), P("pix", "pos")),
        check_vma=False,
    )
```

```python
import math

import jax
import jax.numpy as jnp
from jax import lax
from jax.experimental import pallas as pl
from jax.experimental.pallas import tpu as pltpu
from jax.sharding import PartitionSpec as P

MESH = pl.DeviceIdType.MESH
K = 128
NX = 4
NZ = 8
NP = 8
ROWS = 4096
COLS = 1024
BLOCK = ROWS // NX
CHUNK = BLOCK // NZ
FAR = (4, 3, 5, 2, 6)
RELAYED = (3, 4)
BACK = (2, 6, 3, 5, 4)
LAG = 2
HOME = 1
SIDE = 1
PANEL = 32
HALF_K = K // 2
SCALE = math.sqrt(float(ROWS * NP))
F32 = jnp.float32
BF16 = jnp.bfloat16


def contract(left, right, a, b):
    return lax.dot_general(left, right, (((a,), (b,)), ((), ())), preferred_element_type=F32)


class Places:
    def __init__(self):
        self.pix, self.pos = lax.axis_index("pix"), lax.axis_index("pos")
        self.z, self.x = self.pos // NX, self.pos % NX

    def at_x(self, d):
        return (self.pix, self.z * NX + (self.x + d) % NX)

    def at_z(self, d):
        return (self.pix, ((self.z + d) % NZ) * NX + self.x)

    def at_pix(self, d):
        return ((self.pix + d) % NP, self.pos)

    def block(self, d):
        return (self.x + d) % NX


def send(src, dst, sems, i, where):
    copy = pltpu.make_async_remote_copy(
        src_ref=src, dst_ref=dst, send_sem=sems.at[0, i], recv_sem=sems.at[1, i],
        device_id=where, device_id_type=MESH,
    )
    copy.start()
    return copy


def rows(start, size):
    return pl.ds(pl.multiple_of(start, size), size)


def sum_and_gather(here, compute, consume, part, held, own, relay, across, side, zpart, zgot, full, sems, enter=None):
    def chunk(d):
        return rows((here.z + d) % NZ * CHUNK, CHUNK)

    sides, relays, plus, minus, zs = {}, {}, {}, {}, {}

    def block(b, d):
        held[b] = compute(here.block(d))
        part[b] = held[b].astype(BF16)

    def send_sides(b):
        for k, d in enumerate((1, NZ - 1)):
            sides[b, k] = send(part.at[b, chunk(d)], side.at[b, k], sems, 8 * NZ + 2 * b + k, here.at_z(d))

    def send_plus(i, d):
        plus[i] = send(part.at[1, chunk(d)], across.at[0, i], sems, NZ + i, here.at_x(1))

    def send_minus(i, d):
        minus[i] = send(part.at[2, chunk(d)], across.at[1, i], sems, 2 * NZ + i, here.at_x(3))

    def send_z(d, value):
        zpart[d - 1] = value.astype(BF16)
        zs[d] = send(zpart.at[d - 1], zgot.at[d - 1], sems, 3 * NZ + d, here.at_z(d))

    def arrived(i, d):
        plus[i].wait_recv()
        minus[i].wait_recv()
        value = own[chunk(d), :] + across[0, i].astype(F32) + across[1, i].astype(F32)
        if i not in RELAYED:
            relays[i].wait_recv()
            value = value + across[2, i].astype(F32)
        return value

    block(0, 2)
    if enter is not None:
        enter()
    for i, d in enumerate(FAR):
        if i in RELAYED:
            relays[i] = send(part.at[0, chunk(d)], relay.at[i], sems, i, here.at_x(1 if i % 2 == 0 else 3))
        else:
            relays[i] = send(part.at[0, chunk(d)], across.at[2, i], sems, i, here.at_x(2))
    send_sides(0)
    block(1, 1)
    send_sides(1)
    block(2, 3)
    send_sides(2)
    own[...] = compute(here.block(0))
    for i, d in enumerate(FAR):
        if i % 2 == 1 or i not in RELAYED:
            send_plus(i, d)
        if i % 2 == 0 or i not in RELAYED:
            send_minus(i, d)
    for d in (1, NZ - 1):
        send_z(d, own[chunk(d), :])
    last = len(FAR)
    for step in range(last + LAG):
        if step < last and step in RELAYED:
            d = FAR[step]
            relays[step].wait_recv()
            b = 1 if step % 2 == 0 else 2
            part[b, chunk(d)] = (held[b, chunk(d)] + relay[step].astype(F32)).astype(BF16)
            (send_plus if b == 1 else send_minus)(step, d)
        if step == HOME:
            for b in range(3):
                value = held[b, chunk(0)]
                for k in range(2):
                    sides[b, k].wait_recv()
                    value = value + side[b, k].astype(F32)
                part[b, chunk(0)] = value.astype(BF16)
                if b == 0:
                    relays[last] = send(part.at[0, chunk(0)], across.at[2, last], sems, last, here.at_x(2))
                else:
                    (send_plus if b == 1 else send_minus)(last, 0)
        if step >= LAG:
            send_z(FAR[step - LAG], arrived(step - LAG, FAR[step - LAG]))
    mine = arrived(last, 0)
    for d in range(1, NZ):
        zs[d].wait_recv()
        mine = mine + zgot[d - 1].astype(F32)
    done = [c for group in (sides, relays, plus, minus, zs) for c in group.values()]

    def place(dx, dz):
        return full.at[rows((here.block(dx) * NZ + (here.z + dz) % NZ) * CHUNK, CHUNK)]

    spot = place(0, 0)
    spot[...] = mine.astype(BF16)
    gs, xs, sides = {}, {}, {}

    def send_x(step, dz):
        spot = place(0, dz)
        for d in (2, 1, 3):
            xs[step, d] = send(spot, spot, sems, (4 + d) * NZ + step, here.at_x(d))

    def send_back(d):
        xs[0, d].wait_recv()
        spot = place(NX - d, 0)
        for k, dz in enumerate((1, NZ - 1)):
            sides[d, k] = send(spot, spot, sems, 9 * NZ + 2 * d + k, here.at_z(dz))

    for d in BACK:
        gs[d] = send(spot, spot, sems, 4 * NZ + d, here.at_z(d))
    send_x(0, 0)
    for d in (1, NZ - 1):
        gs[d] = send(spot, spot, sems, 4 * NZ + d, here.at_z(d))
    for step, d in enumerate(BACK):
        gs[NZ - d].wait_recv()
        send_x(step + 1, d)
        if step == SIDE:
            send_back(1)
            send_back(3)
        if step == SIDE + 1:
            send_back(2)
    for d in (1, NZ - 1):
        gs[d].wait_recv()
    consume(here.block(0))
    for d in (1, 3, 2):
        for step in range(1, len(BACK) + 1):
            xs[step, d].wait_recv()
        for k in range(2):
            sides[d, k].wait_recv()
        consume(here.block(NX - d))
    return done + [c for group in (gs, xs, sides) for c in group.values()]


def inverse_factor(gram):
    ids = lax.broadcasted_iota(jnp.int32, (K, K), 0)
    a, v = gram, (ids == lax.broadcasted_iota(jnp.int32, (K, K), 1)).astype(F32)
    row = lax.broadcasted_iota(jnp.int32, (PANEL, K), 0)
    out = []
    for lo in range(0, K, PANEL):
        ap, vp = a[:PANEL], v[:PANEL]
        c = jnp.stack([jnp.broadcast_to(ap[:, lo + k:lo + k + 1], (PANEL, K)) for k in range(PANEL)])
        for j in range(PANEL):
            r = lax.rsqrt(jnp.broadcast_to(c[0, j:j + 1], (PANEL, K)))
            below = jnp.where(row > j, c[0] * r, 0.0)
            ra, rv = ap[j:j + 1] * r, vp[j:j + 1] * r
            ap = jnp.where(row == j, ra, ap - below * ra)
            vp = jnp.where(row == j, rv, vp - below * rv)
            if j + 1 < PANEL:
                c = c[1:]
                c = c - below[None] * (c[:, j:j + 1, :] * r[None])
        out.append(vp)
        if lo + PANEL < K:
            both = lax.dot_general(
                ap, jnp.concatenate([ap, vp], axis=1), (((0,), (0,)), ((), ())),
                precision=lax.Precision.HIGHEST, preferred_element_type=F32,
            )
            a = a[PANEL:] - both[lo + PANEL:, :K]
            v = v[PANEL:] - both[lo + PANEL:, K:]
    return jnp.concatenate(out, axis=0)


def thirds(value):
    top = value.astype(BF16)
    rest = value - top.astype(F32)
    mid = rest.astype(BF16)
    return top, mid, (rest - mid.astype(F32)).astype(BF16)


def whole_kernel(
    stack, omega, basis_out, projected_out,
    m, om, test, part, held, own, relay, across, side, zpart, zgot, full,
    bt, bparts, bgot, back, total, mine_gram, half_got, halves, gram, factor, pparts, pgot, pall,
    load_sems, sems, pix_sems, gram_sems,
):
    here = Places()
    barrier = pltpu.get_barrier_semaphore()
    partners = [here.at_x(d) for d in range(1, NX)]
    partners += [here.at_z(d) for d in range(1, NZ)] + [here.at_pix(d) for d in range(1, NP)]
    for p in partners:
        pl.semaphore_signal(barrier, inc=1, device_id=p, device_id_type=MESH)
    load_om = pltpu.make_async_copy(omega, om, load_sems.at[4])
    load_om.start()
    flat = stack.reshape(ROWS, COLS)
    loads = []
    for i, d in enumerate((2, 1, 3, 0)):
        where = rows(here.block(d) * BLOCK, BLOCK)
        loads.append(pltpu.make_async_copy(flat.at[where], m.at[where], load_sems.at[i]))
        loads[i].start()
    load_om.wait()
    test[...] = (om[...].astype(F32) / 32768.0).astype(BF16)
    turn = iter(loads)

    def first_block(b):
        next(turn).wait()
        return jnp.dot(m[rows(b * BLOCK, BLOCK), :], test[...], preferred_element_type=F32)

    def take_first(b):
        where = rows(b * BLOCK, BLOCK)
        bt[...] += contract(full[0, where, :], m[where, :], 0, 0)

    bt[...] = jnp.zeros_like(bt)
    copies = sum_and_gather(
        here, first_block, take_first, part.at[0], held, own, relay.at[0],
        across.at[0], side.at[0], zpart.at[0], zgot.at[0], full.at[0], sems.at[0],
        lambda: pl.semaphore_wait(barrier, len(partners)),
    )

    for j in range(NP):
        bparts[j] = bt[:, j * K:(j + 1) * K].astype(BF16)
        total[j] = bt[:, j * K:(j + 1) * K]
    bs = []
    for d in range(1, NP):
        bs.append(send(bparts.at[(here.pix + d) % NP], bgot.at[d - 1], pix_sems.at[0], d - 1, here.at_pix(d)))
    mine = total[here.pix]
    for d in range(1, NP):
        bs[d - 1].wait_recv()
        mine = mine + bgot[d - 1].astype(F32)
    spot = back.at[rows(here.pix * K, K)]
    spot[...] = mine.T.astype(BF16)
    gs = [send(spot, spot, pix_sems.at[1], d - 1, here.at_pix(d)) for d in range(1, NP)]
    for c in gs:
        c.wait_recv()
    copies += bs + gs

    def sketch_block(b):
        return jnp.dot(m[rows(b * BLOCK, BLOCK), :], back[...], preferred_element_type=F32)

    def take_sketch(b):
        where = rows(b * BLOCK, BLOCK)
        s = full[1, where, :]
        total[b] = contract(s, s, 0, 0)
        bt[...] += contract(s, m[where, :], 0, 0)

    bt[...] = jnp.zeros_like(bt)
    copies += sum_and_gather(
        here, sketch_block, take_sketch, part.at[1], held, own, relay.at[1],
        across.at[1], side.at[1], zpart.at[1], zgot.at[1], full.at[1], sems.at[1],
    )

    y, core = here.pix // 2, here.pix % 2
    near = (y * 2 + 1 - core, here.pos)
    mine_gram[...] = total[0] + total[1] + total[2] + total[3]
    keep, give = rows(core * HALF_K, HALF_K), rows((1 - core) * HALF_K, HALF_K)
    swap = send(mine_gram.at[give], half_got, gram_sems, 0, near)
    swap.wait_recv()
    halves[y] = mine_gram[keep, :] + half_got[...]
    spot = halves.at[y]
    ys = [send(spot, spot, gram_sems, d, ((y + d) % 4 * 2 + core, here.pos)) for d in (1, 2, 3)]
    for j in range(NP):
        pparts[j] = bt[:, j * K:(j + 1) * K].astype(BF16)
        total[j] = bt[:, j * K:(j + 1) * K]
    ps = []
    for d in range(1, NP):
        ps.append(send(pparts.at[(here.pix + d) % NP], pgot.at[d - 1], pix_sems.at[2], d - 1, here.at_pix(d)))
    for c in ys:
        c.wait_recv()
    gram[keep, :] = (halves[0] + halves[1]) + (halves[2] + halves[3])
    spot = gram.at[keep]
    swap_back = send(spot, spot, gram_sems, 4, near)
    mine = total[here.pix]
    for d in range(1, NP):
        ps[d - 1].wait_recv()
        mine = mine + pgot[d - 1].astype(F32)
    pall[here.pix] = mine.astype(BF16)
    spot = pall.at[here.pix]
    gs = [send(spot, spot, pix_sems.at[3], d - 1, here.at_pix(d)) for d in range(1, NP)]
    swap_back.wait_recv()
    copies += [swap, swap_back] + ys + ps + gs
    inverse = inverse_factor(gram[...])
    factor[...] = inverse

    scaled = inverse.T * SCALE
    top, mid, low = thirds(scaled)
    for b in range(NX):
        where = pl.ds(b * BLOCK, BLOCK)
        s = full[1, where, :]
        basis_out[where, :] = (
            jnp.dot(s, top, preferred_element_type=F32)
            + jnp.dot(s, mid, preferred_element_type=F32)
            + jnp.dot(s, low, preferred_element_type=F32)
        )
    share = K // NP
    lines = jnp.concatenate(thirds(factor[rows(here.pix * share, share), :]), axis=0)
    for c in gs:
        c.wait_recv()
    for j in range(NP):
        product = jnp.dot(lines, pall[j], preferred_element_type=F32)
        projected_out[:, j * K:(j + 1) * K] = product[:share] + product[share:2 * share] + product[2 * share:]
    for c in copies:
        c.wait_send()


def body(stack, omega):
    vmem = pl.BlockSpec(memory_space=pltpu.VMEM)
    hbm = pl.BlockSpec(memory_space=pl.ANY)
    basis, projected = pl.pallas_call(
        whole_kernel,
        out_shape=(
            jax.ShapeDtypeStruct((ROWS, K), F32),
            jax.ShapeDtypeStruct((K // NP, COLS), F32),
        ),
        in_specs=[hbm, pl.BlockSpec(memory_space=pltpu.HBM)],
        out_specs=(vmem, vmem),
        scratch_shapes=[
            pltpu.VMEM((ROWS, COLS), BF16),
            pltpu.VMEM((COLS, K), jnp.int32),
            pltpu.VMEM((COLS, K), BF16),
            pltpu.VMEM((2, 3, BLOCK, K), BF16),
            pltpu.VMEM((3, BLOCK, K), F32),
            pltpu.VMEM((BLOCK, K), F32),
            pltpu.VMEM((2, NZ, CHUNK, K), BF16),
            pltpu.VMEM((2, 3, NZ, CHUNK, K), BF16),
            pltpu.VMEM((2, 3, 2, CHUNK, K), BF16),
            pltpu.VMEM((2, NZ - 1, CHUNK, K), BF16),
            pltpu.VMEM((2, NZ - 1, CHUNK, K), BF16),
            pltpu.VMEM((2, ROWS, K), BF16),
            pltpu.VMEM((K, COLS), F32),
            pltpu.VMEM((NP, K, K), BF16),
            pltpu.VMEM((NP - 1, K, K), BF16),
            pltpu.VMEM((COLS, K), BF16),
            pltpu.VMEM((NP, K, K), F32),
            pltpu.VMEM((K, K), F32),
            pltpu.VMEM((HALF_K, K), F32),
            pltpu.VMEM((4, HALF_K, K), F32),
            pltpu.VMEM((K, K), F32),
            pltpu.VMEM((K, K), F32),
            pltpu.VMEM((NP, K, K), BF16),
            pltpu.VMEM((NP - 1, K, K), BF16),
            pltpu.VMEM((NP, K, K), BF16),
            pltpu.SemaphoreType.DMA((5,)),
            pltpu.SemaphoreType.DMA((2, 2, 10 * NZ)),
            pltpu.SemaphoreType.DMA((4, 2, NP - 1)),
            pltpu.SemaphoreType.DMA((2, 5)),
        ],
        compiler_params=pltpu.CompilerParams(
            collective_id=0, has_side_effects=True, vmem_limit_bytes=48 << 20
        ),
        cost_estimate=pl.CostEstimate(flops=4 * 2 * ROWS * COLS * K, bytes_accessed=12 << 20, transcendentals=0),
    )(stack, omega)
    return basis.reshape(stack.shape[0], 2, K), projected


def solution(mesh):
    return jax.shard_map(
        body,
        mesh=mesh,
        in_specs=(P("pix", None, "pos"), P("pos", None)),
        out_specs=(P("pix", None, None), P("pix", "pos")),
        check_vma=False,
    )
```

```python
import math

import jax
import jax.numpy as jnp
from jax import lax
from jax.experimental import pallas as pl
from jax.experimental.pallas import tpu as pltpu
from jax.sharding import PartitionSpec as P

MESH = pl.DeviceIdType.MESH
K = 128
NX = 4
NZ = 8
NP = 8
ROWS = 4096
COLS = 1024
BLOCK = ROWS // NX
CHUNK = BLOCK // NZ
FAR = (4, 3, 5, 2, 6)
RELAYED = (3, 4)
BACK = (2, 6, 3, 5, 4)
LAG = 2
HOME = 1
SIDE = 1
PIX_ORDER = (4, 3, 5, 2, 6, 1, 7)
PANEL = 32
HALF_K = K // 2
SCALE = math.sqrt(float(ROWS * NP))
F32 = jnp.float32
BF16 = jnp.bfloat16


def contract(left, right, a, b):
    return lax.dot_general(left, right, (((a,), (b,)), ((), ())), preferred_element_type=F32)


class Places:
    def __init__(self):
        self.pix, self.pos = lax.axis_index("pix"), lax.axis_index("pos")
        self.z, self.x = self.pos // NX, self.pos % NX

    def at_x(self, d):
        return (self.pix, self.z * NX + (self.x + d) % NX)

    def at_z(self, d):
        return (self.pix, ((self.z + d) % NZ) * NX + self.x)

    def at_pix(self, d):
        return ((self.pix + d) % NP, self.pos)

    def block(self, d):
        return (self.x + d) % NX


def send(src, dst, sems, i, where):
    copy = pltpu.make_async_remote_copy(
        src_ref=src, dst_ref=dst, send_sem=sems.at[0, i], recv_sem=sems.at[1, i],
        device_id=where, device_id_type=MESH,
    )
    copy.start()
    return copy


def rows(start, size):
    return pl.ds(pl.multiple_of(start, size), size)


def sum_and_gather(here, compute, consume, part, held, own, relay, across, side, zpart, zgot, full, sems, enter=None):
    def chunk(d):
        return rows((here.z + d) % NZ * CHUNK, CHUNK)

    sides, relays, plus, minus, zs = {}, {}, {}, {}, {}

    def block(b, d):
        held[b] = compute(here.block(d))
        part[b] = held[b].astype(BF16)

    def send_sides(b):
        for k, d in enumerate((1, NZ - 1)):
            sides[b, k] = send(part.at[b, chunk(d)], side.at[b, k], sems, 8 * NZ + 2 * b + k, here.at_z(d))

    def send_plus(i, d):
        plus[i] = send(part.at[1, chunk(d)], across.at[0, i], sems, NZ + i, here.at_x(1))

    def send_minus(i, d):
        minus[i] = send(part.at[2, chunk(d)], across.at[1, i], sems, 2 * NZ + i, here.at_x(3))

    def send_z(d, value):
        zpart[d - 1] = value.astype(BF16)
        zs[d] = send(zpart.at[d - 1], zgot.at[d - 1], sems, 3 * NZ + d, here.at_z(d))

    def arrived(i, d):
        plus[i].wait_recv()
        minus[i].wait_recv()
        value = own[chunk(d), :] + across[0, i].astype(F32) + across[1, i].astype(F32)
        if i not in RELAYED:
            relays[i].wait_recv()
            value = value + across[2, i].astype(F32)
        return value

    block(0, 2)
    if enter is not None:
        enter()
    for i, d in enumerate(FAR):
        if i in RELAYED:
            relays[i] = send(part.at[0, chunk(d)], relay.at[i], sems, i, here.at_x(1 if i % 2 == 0 else 3))
        else:
            relays[i] = send(part.at[0, chunk(d)], across.at[2, i], sems, i, here.at_x(2))
    send_sides(0)
    block(1, 1)
    send_sides(1)
    block(2, 3)
    send_sides(2)
    own[...] = compute(here.block(0))
    for i, d in enumerate(FAR):
        if i % 2 == 1 or i not in RELAYED:
            send_plus(i, d)
        if i % 2 == 0 or i not in RELAYED:
            send_minus(i, d)
    for d in (1, NZ - 1):
        send_z(d, own[chunk(d), :])
    last = len(FAR)
    for step in range(last + LAG):
        if step < last and step in RELAYED:
            d = FAR[step]
            relays[step].wait_recv()
            b = 1 if step % 2 == 0 else 2
            part[b, chunk(d)] = (held[b, chunk(d)] + relay[step].astype(F32)).astype(BF16)
            (send_plus if b == 1 else send_minus)(step, d)
        if step == HOME:
            for b in range(3):
                value = held[b, chunk(0)]
                for k in range(2):
                    sides[b, k].wait_recv()
                    value = value + side[b, k].astype(F32)
                part[b, chunk(0)] = value.astype(BF16)
                if b == 0:
                    relays[last] = send(part.at[0, chunk(0)], across.at[2, last], sems, last, here.at_x(2))
                else:
                    (send_plus if b == 1 else send_minus)(last, 0)
        if step >= LAG:
            send_z(FAR[step - LAG], arrived(step - LAG, FAR[step - LAG]))
    mine = arrived(last, 0)
    for d in range(1, NZ):
        zs[d].wait_recv()
        mine = mine + zgot[d - 1].astype(F32)
    done = [c for group in (sides, relays, plus, minus, zs) for c in group.values()]

    def place(dx, dz):
        return full.at[rows((here.block(dx) * NZ + (here.z + dz) % NZ) * CHUNK, CHUNK)]

    spot = place(0, 0)
    spot[...] = mine.astype(BF16)
    gs, xs, sides = {}, {}, {}

    def send_x(step, dz):
        spot = place(0, dz)
        for d in (2, 1, 3):
            xs[step, d] = send(spot, spot, sems, (4 + d) * NZ + step, here.at_x(d))

    def send_back(d):
        xs[0, d].wait_recv()
        spot = place(NX - d, 0)
        for k, dz in enumerate((1, NZ - 1)):
            sides[d, k] = send(spot, spot, sems, 9 * NZ + 2 * d + k, here.at_z(dz))

    for d in BACK:
        gs[d] = send(spot, spot, sems, 4 * NZ + d, here.at_z(d))
    send_x(0, 0)
    for d in (1, NZ - 1):
        gs[d] = send(spot, spot, sems, 4 * NZ + d, here.at_z(d))
    for step, d in enumerate(BACK):
        gs[NZ - d].wait_recv()
        send_x(step + 1, d)
        if step == SIDE:
            send_back(1)
            send_back(3)
        if step == SIDE + 1:
            send_back(2)
    for d in (1, NZ - 1):
        gs[d].wait_recv()
    consume(here.block(0))
    for d in (1, 3, 2):
        for step in range(1, len(BACK) + 1):
            xs[step, d].wait_recv()
        for k in range(2):
            sides[d, k].wait_recv()
        consume(here.block(NX - d))
    return done + [c for group in (gs, xs, sides) for c in group.values()]


def inverse_factor(gram):
    ids = lax.broadcasted_iota(jnp.int32, (K, K), 0)
    a, v = gram, (ids == lax.broadcasted_iota(jnp.int32, (K, K), 1)).astype(F32)
    row = lax.broadcasted_iota(jnp.int32, (PANEL, K), 0)
    out = []
    for lo in range(0, K, PANEL):
        ap, vp = a[:PANEL], v[:PANEL]
        c = jnp.stack([jnp.broadcast_to(ap[:, lo + k:lo + k + 1], (PANEL, K)) for k in range(PANEL)])
        for j in range(PANEL):
            r = lax.rsqrt(jnp.broadcast_to(c[0, j:j + 1], (PANEL, K)))
            below = jnp.where(row > j, c[0] * r, 0.0)
            ra, rv = ap[j:j + 1] * r, vp[j:j + 1] * r
            ap = jnp.where(row == j, ra, ap - below * ra)
            vp = jnp.where(row == j, rv, vp - below * rv)
            if j + 1 < PANEL:
                c = c[1:]
                c = c - below[None] * (c[:, j:j + 1, :] * r[None])
        out.append(vp)
        if lo + PANEL < K:
            both = lax.dot_general(
                ap, jnp.concatenate([ap, vp], axis=1), (((0,), (0,)), ((), ())),
                precision=lax.Precision.HIGHEST, preferred_element_type=F32,
            )
            a = a[PANEL:] - both[lo + PANEL:, :K]
            v = v[PANEL:] - both[lo + PANEL:, K:]
    return jnp.concatenate(out, axis=0)


def thirds(value):
    top = value.astype(BF16)
    rest = value - top.astype(F32)
    mid = rest.astype(BF16)
    return top, mid, (rest - mid.astype(F32)).astype(BF16)


def whole_kernel(
    stack, omega, basis_out, projected_out,
    m, om, test, part, held, own, relay, across, side, zpart, zgot, full,
    bt, bparts, bgot, back, total, mine_gram, half_got, halves, gram, factor, pparts, pgot, pall,
    load_sems, sems, pix_sems, gram_sems,
):
    here = Places()
    barrier = pltpu.get_barrier_semaphore()
    partners = [here.at_x(d) for d in range(1, NX)]
    partners += [here.at_z(d) for d in range(1, NZ)] + [here.at_pix(d) for d in range(1, NP)]
    for p in partners:
        pl.semaphore_signal(barrier, inc=1, device_id=p, device_id_type=MESH)
    load_om = pltpu.make_async_copy(omega, om, load_sems.at[4])
    load_om.start()
    flat = stack.reshape(ROWS, COLS)
    loads = []
    for i, d in enumerate((2, 1, 3, 0)):
        where = rows(here.block(d) * BLOCK, BLOCK)
        loads.append(pltpu.make_async_copy(flat.at[where], m.at[where], load_sems.at[i]))
        loads[i].start()
    load_om.wait()
    test[...] = (om[...].astype(F32) / 32768.0).astype(BF16)
    turn = iter(loads)

    def first_block(b):
        next(turn).wait()
        return jnp.dot(m[rows(b * BLOCK, BLOCK), :], test[...], preferred_element_type=F32)

    def take_first(b):
        where = rows(b * BLOCK, BLOCK)
        bt[...] += contract(full[0, where, :], m[where, :], 0, 0)

    bt[...] = jnp.zeros_like(bt)
    copies = sum_and_gather(
        here, first_block, take_first, part.at[0], held, own, relay.at[0],
        across.at[0], side.at[0], zpart.at[0], zgot.at[0], full.at[0], sems.at[0],
        lambda: pl.semaphore_wait(barrier, len(partners)),
    )

    for j in range(NP):
        bparts[j] = bt[:, j * K:(j + 1) * K].astype(BF16)
        total[j] = bt[:, j * K:(j + 1) * K]
    bs = {}
    for d in PIX_ORDER:
        bs[d] = send(bparts.at[(here.pix + d) % NP], bgot.at[d - 1], pix_sems.at[0], d - 1, here.at_pix(d))
    mine = total[here.pix]
    for d in range(1, NP):
        bs[d].wait_recv()
        mine = mine + bgot[d - 1].astype(F32)
    spot = back.at[rows(here.pix * K, K)]
    spot[...] = mine.T.astype(BF16)
    gs = [send(spot, spot, pix_sems.at[1], d - 1, here.at_pix(d)) for d in PIX_ORDER]
    for c in gs:
        c.wait_recv()
    copies += list(bs.values()) + gs

    def sketch_block(b):
        return jnp.dot(m[rows(b * BLOCK, BLOCK), :], back[...], preferred_element_type=F32)

    def take_sketch(b):
        where = rows(b * BLOCK, BLOCK)
        s = full[1, where, :]
        total[b] = contract(s, s, 0, 0)
        bt[...] += contract(s, m[where, :], 0, 0)

    bt[...] = jnp.zeros_like(bt)
    copies += sum_and_gather(
        here, sketch_block, take_sketch, part.at[1], held, own, relay.at[1],
        across.at[1], side.at[1], zpart.at[1], zgot.at[1], full.at[1], sems.at[1],
    )

    y, core = here.pix // 2, here.pix % 2
    near = (y * 2 + 1 - core, here.pos)
    mine_gram[...] = total[0] + total[1] + total[2] + total[3]
    keep, give = rows(core * HALF_K, HALF_K), rows((1 - core) * HALF_K, HALF_K)
    swap = send(mine_gram.at[give], half_got, gram_sems, 0, near)
    swap.wait_recv()
    halves[y] = mine_gram[keep, :] + half_got[...]
    spot = halves.at[y]
    ys = [send(spot, spot, gram_sems, d, ((y + d) % 4 * 2 + core, here.pos)) for d in (1, 2, 3)]
    for j in range(NP):
        pparts[j] = bt[:, j * K:(j + 1) * K].astype(BF16)
        total[j] = bt[:, j * K:(j + 1) * K]
    ps = {}
    for d in PIX_ORDER:
        ps[d] = send(pparts.at[(here.pix + d) % NP], pgot.at[d - 1], pix_sems.at[2], d - 1, here.at_pix(d))
    for c in ys:
        c.wait_recv()
    gram[keep, :] = (halves[0] + halves[1]) + (halves[2] + halves[3])
    spot = gram.at[keep]
    swap_back = send(spot, spot, gram_sems, 4, near)
    mine = total[here.pix]
    for d in range(1, NP):
        ps[d].wait_recv()
        mine = mine + pgot[d - 1].astype(F32)
    pall[here.pix] = mine.astype(BF16)
    spot = pall.at[here.pix]
    gs = [send(spot, spot, pix_sems.at[3], d - 1, here.at_pix(d)) for d in PIX_ORDER]
    swap_back.wait_recv()
    copies += [swap, swap_back] + ys + list(ps.values()) + gs
    inverse = inverse_factor(gram[...])
    factor[...] = inverse

    scaled = inverse.T * SCALE
    top, mid, low = thirds(scaled)
    for b in range(NX):
        where = pl.ds(b * BLOCK, BLOCK)
        s = full[1, where, :]
        basis_out[where, :] = (
            jnp.dot(s, top, preferred_element_type=F32)
            + jnp.dot(s, mid, preferred_element_type=F32)
            + jnp.dot(s, low, preferred_element_type=F32)
        )
    share = K // NP
    lines = jnp.concatenate(thirds(factor[rows(here.pix * share, share), :]), axis=0)
    for c in gs:
        c.wait_recv()
    for j in range(NP):
        product = jnp.dot(lines, pall[j], preferred_element_type=F32)
        projected_out[:, j * K:(j + 1) * K] = product[:share] + product[share:2 * share] + product[2 * share:]
    for c in copies:
        c.wait_send()


def body(stack, omega):
    vmem = pl.BlockSpec(memory_space=pltpu.VMEM)
    hbm = pl.BlockSpec(memory_space=pl.ANY)
    basis, projected = pl.pallas_call(
        whole_kernel,
        out_shape=(
            jax.ShapeDtypeStruct((ROWS, K), F32),
            jax.ShapeDtypeStruct((K // NP, COLS), F32),
        ),
        in_specs=[hbm, pl.BlockSpec(memory_space=pltpu.HBM)],
        out_specs=(vmem, vmem),
        scratch_shapes=[
            pltpu.VMEM((ROWS, COLS), BF16),
            pltpu.VMEM((COLS, K), jnp.int32),
            pltpu.VMEM((COLS, K), BF16),
            pltpu.VMEM((2, 3, BLOCK, K), BF16),
            pltpu.VMEM((3, BLOCK, K), F32),
            pltpu.VMEM((BLOCK, K), F32),
            pltpu.VMEM((2, NZ, CHUNK, K), BF16),
            pltpu.VMEM((2, 3, NZ, CHUNK, K), BF16),
            pltpu.VMEM((2, 3, 2, CHUNK, K), BF16),
            pltpu.VMEM((2, NZ - 1, CHUNK, K), BF16),
            pltpu.VMEM((2, NZ - 1, CHUNK, K), BF16),
            pltpu.VMEM((2, ROWS, K), BF16),
            pltpu.VMEM((K, COLS), F32),
            pltpu.VMEM((NP, K, K), BF16),
            pltpu.VMEM((NP - 1, K, K), BF16),
            pltpu.VMEM((COLS, K), BF16),
            pltpu.VMEM((NP, K, K), F32),
            pltpu.VMEM((K, K), F32),
            pltpu.VMEM((HALF_K, K), F32),
            pltpu.VMEM((4, HALF_K, K), F32),
            pltpu.VMEM((K, K), F32),
            pltpu.VMEM((K, K), F32),
            pltpu.VMEM((NP, K, K), BF16),
            pltpu.VMEM((NP - 1, K, K), BF16),
            pltpu.VMEM((NP, K, K), BF16),
            pltpu.SemaphoreType.DMA((5,)),
            pltpu.SemaphoreType.DMA((2, 2, 10 * NZ)),
            pltpu.SemaphoreType.DMA((4, 2, NP - 1)),
            pltpu.SemaphoreType.DMA((2, 5)),
        ],
        compiler_params=pltpu.CompilerParams(
            collective_id=0, has_side_effects=True, vmem_limit_bytes=48 << 20
        ),
        cost_estimate=pl.CostEstimate(flops=4 * 2 * ROWS * COLS * K, bytes_accessed=12 << 20, transcendentals=0),
    )(stack, omega)
    return basis.reshape(stack.shape[0], 2, K), projected


def solution(mesh):
    return jax.shard_map(
        body,
        mesh=mesh,
        in_specs=(P("pix", None, "pos"), P("pos", None)),
        out_specs=(P("pix", None, None), P("pix", "pos")),
        check_vma=False,
    )
```

```python
import math

import jax
import jax.numpy as jnp
from jax import lax
from jax.experimental import pallas as pl
from jax.experimental.pallas import tpu as pltpu
from jax.sharding import PartitionSpec as P

MESH = pl.DeviceIdType.MESH
K = 128
NX = 4
NZ = 8
NP = 8
ROWS = 4096
COLS = 1024
BLOCK = ROWS // NX
CHUNK = BLOCK // NZ
FAR = (4, 3, 5, 2, 6)
RELAYED = (3, 4)
BACK = (2, 6, 3, 5, 4)
LAG = 2
HOME = 1
SIDE = 1
PIX_ORDER = (4, 3, 5, 2, 6, 1, 7)
PANEL = 32
HALF_K = K // 2
SCALE = math.sqrt(float(ROWS * NP))
F32 = jnp.float32
BF16 = jnp.bfloat16


def contract(left, right, a, b):
    return lax.dot_general(left, right, (((a,), (b,)), ((), ())), preferred_element_type=F32)


class Places:
    def __init__(self):
        self.pix, self.pos = lax.axis_index("pix"), lax.axis_index("pos")
        self.z, self.x = self.pos // NX, self.pos % NX

    def at_x(self, d):
        return (self.pix, self.z * NX + (self.x + d) % NX)

    def at_z(self, d):
        return (self.pix, ((self.z + d) % NZ) * NX + self.x)

    def at_pix(self, d):
        return ((self.pix + d) % NP, self.pos)

    def block(self, d):
        return (self.x + d) % NX


def send(src, dst, sems, i, where):
    copy = pltpu.make_async_remote_copy(
        src_ref=src, dst_ref=dst, send_sem=sems.at[0, i], recv_sem=sems.at[1, i],
        device_id=where, device_id_type=MESH,
    )
    copy.start()
    return copy


def rows(start, size):
    return pl.ds(pl.multiple_of(start, size), size)


def sum_and_gather(here, compute, consume, part, held, own, relay, across, side, zpart, zgot, full, sems, enter=None):
    def chunk(d):
        return rows((here.z + d) % NZ * CHUNK, CHUNK)

    sides, relays, plus, minus, zs = {}, {}, {}, {}, {}

    def block(b, d):
        held[b] = compute(here.block(d))
        part[b] = held[b].astype(BF16)

    def send_sides(b):
        for k, d in enumerate((1, NZ - 1)):
            sides[b, k] = send(part.at[b, chunk(d)], side.at[b, k], sems, 8 * NZ + 2 * b + k, here.at_z(d))

    def send_plus(i, d):
        plus[i] = send(part.at[1, chunk(d)], across.at[0, i], sems, NZ + i, here.at_x(1))

    def send_minus(i, d):
        minus[i] = send(part.at[2, chunk(d)], across.at[1, i], sems, 2 * NZ + i, here.at_x(3))

    def send_z(d, value):
        zpart[d - 1] = value.astype(BF16)
        zs[d] = send(zpart.at[d - 1], zgot.at[d - 1], sems, 3 * NZ + d, here.at_z(d))

    def arrived(i, d):
        plus[i].wait_recv()
        minus[i].wait_recv()
        value = own[chunk(d), :] + across[0, i].astype(F32) + across[1, i].astype(F32)
        if i not in RELAYED:
            relays[i].wait_recv()
            value = value + across[2, i].astype(F32)
        return value

    block(0, 2)
    if enter is not None:
        enter()
    for i, d in enumerate(FAR):
        if i in RELAYED:
            relays[i] = send(part.at[0, chunk(d)], relay.at[i], sems, i, here.at_x(1 if i % 2 == 0 else 3))
        else:
            relays[i] = send(part.at[0, chunk(d)], across.at[2, i], sems, i, here.at_x(2))
    send_sides(0)
    block(1, 1)
    send_sides(1)
    block(2, 3)
    send_sides(2)
    own[...] = compute(here.block(0))
    for i, d in enumerate(FAR):
        if i % 2 == 1 or i not in RELAYED:
            send_plus(i, d)
        if i % 2 == 0 or i not in RELAYED:
            send_minus(i, d)
    for d in (1, NZ - 1):
        send_z(d, own[chunk(d), :])
    last = len(FAR)
    for step in range(last + LAG):
        if step < last and step in RELAYED:
            d = FAR[step]
            relays[step].wait_recv()
            b = 1 if step % 2 == 0 else 2
            part[b, chunk(d)] = (held[b, chunk(d)] + relay[step].astype(F32)).astype(BF16)
            (send_plus if b == 1 else send_minus)(step, d)
        if step == HOME:
            for b in range(3):
                value = held[b, chunk(0)]
                for k in range(2):
                    sides[b, k].wait_recv()
                    value = value + side[b, k].astype(F32)
                part[b, chunk(0)] = value.astype(BF16)
                if b == 0:
                    relays[last] = send(part.at[0, chunk(0)], across.at[2, last], sems, last, here.at_x(2))
                else:
                    (send_plus if b == 1 else send_minus)(last, 0)
        if step >= LAG:
            send_z(FAR[step - LAG], arrived(step - LAG, FAR[step - LAG]))
    mine = arrived(last, 0)
    for d in range(1, NZ):
        zs[d].wait_recv()
        mine = mine + zgot[d - 1].astype(F32)
    done = [c for group in (sides, relays, plus, minus, zs) for c in group.values()]

    def place(dx, dz):
        return full.at[rows((here.block(dx) * NZ + (here.z + dz) % NZ) * CHUNK, CHUNK)]

    spot = place(0, 0)
    spot[...] = mine.astype(BF16)
    gs, xs, sides = {}, {}, {}

    def send_x(step, dz):
        spot = place(0, dz)
        for d in (2, 1, 3):
            xs[step, d] = send(spot, spot, sems, (4 + d) * NZ + step, here.at_x(d))

    def send_back(d):
        xs[0, d].wait_recv()
        spot = place(NX - d, 0)
        for k, dz in enumerate((1, NZ - 1)):
            sides[d, k] = send(spot, spot, sems, 9 * NZ + 2 * d + k, here.at_z(dz))

    for d in BACK:
        gs[d] = send(spot, spot, sems, 4 * NZ + d, here.at_z(d))
    send_x(0, 0)
    for d in (1, NZ - 1):
        gs[d] = send(spot, spot, sems, 4 * NZ + d, here.at_z(d))
    for step, d in enumerate(BACK):
        gs[NZ - d].wait_recv()
        send_x(step + 1, d)
        if step == SIDE:
            send_back(1)
            send_back(3)
        if step == SIDE + 1:
            send_back(2)
    for d in (1, NZ - 1):
        gs[d].wait_recv()
    consume(here.block(0))
    for d in (1, 3, 2):
        for step in range(1, len(BACK) + 1):
            xs[step, d].wait_recv()
        for k in range(2):
            sides[d, k].wait_recv()
        consume(here.block(NX - d))
    return done + [c for group in (gs, xs, sides) for c in group.values()]


def inverse_factor(gram):
    ids = lax.broadcasted_iota(jnp.int32, (K, K), 0)
    a, v = gram, (ids == lax.broadcasted_iota(jnp.int32, (K, K), 1)).astype(F32)
    row = lax.broadcasted_iota(jnp.int32, (PANEL, K), 0)
    out = []
    for lo in range(0, K, PANEL):
        ap, vp = a[:PANEL], v[:PANEL]
        c = jnp.stack([jnp.broadcast_to(ap[:, lo + k:lo + k + 1], (PANEL, K)) for k in range(PANEL)])
        for j in range(PANEL):
            r = lax.rsqrt(jnp.broadcast_to(c[0, j:j + 1], (PANEL, K)))
            below = jnp.where(row > j, c[0] * r, 0.0)
            ra, rv = ap[j:j + 1] * r, vp[j:j + 1] * r
            ap = jnp.where(row == j, ra, ap - below * ra)
            vp = jnp.where(row == j, rv, vp - below * rv)
            if j + 1 < PANEL:
                c = c[1:]
                c = c - below[None] * (c[:, j:j + 1, :] * r[None])
        out.append(vp)
        if lo + PANEL < K:
            both = lax.dot_general(
                ap, jnp.concatenate([ap, vp], axis=1), (((0,), (0,)), ((), ())),
                precision=lax.Precision.HIGHEST, preferred_element_type=F32,
            )
            a = a[PANEL:] - both[lo + PANEL:, :K]
            v = v[PANEL:] - both[lo + PANEL:, K:]
    return jnp.concatenate(out, axis=0)


def thirds(value):
    top = value.astype(BF16)
    rest = value - top.astype(F32)
    mid = rest.astype(BF16)
    return top, mid, (rest - mid.astype(F32)).astype(BF16)


def whole_kernel(
    stack, omega, basis_out, projected_out,
    m, om, test, part, held, own, relay, across, side, zpart, zgot, full,
    bt, bparts, bgot, back, total, mine_gram, half_got, halves, gram, factor, pparts, pgot, pall,
    load_sems, sems, pix_sems, gram_sems,
):
    here = Places()
    barrier = pltpu.get_barrier_semaphore()
    partners = [here.at_x(d) for d in range(1, NX)]
    partners += [here.at_z(d) for d in range(1, NZ)] + [here.at_pix(d) for d in range(1, NP)]
    for p in partners:
        pl.semaphore_signal(barrier, inc=1, device_id=p, device_id_type=MESH)
    load_om = pltpu.make_async_copy(omega, om, load_sems.at[4])
    load_om.start()
    flat = stack.reshape(ROWS, COLS)
    loads = []
    for i, d in enumerate((2, 1, 3, 0)):
        where = rows(here.block(d) * BLOCK, BLOCK)
        loads.append(pltpu.make_async_copy(flat.at[where], m.at[where], load_sems.at[i]))
        loads[i].start()
    load_om.wait()
    test[...] = (om[...].astype(F32) / 32768.0).astype(BF16)
    turn = iter(loads)

    def first_block(b):
        next(turn).wait()
        return jnp.dot(m[rows(b * BLOCK, BLOCK), :], test[...], preferred_element_type=F32)

    def take_first(b):
        where = rows(b * BLOCK, BLOCK)
        bt[...] += contract(full[0, where, :], m[where, :], 0, 0)

    bt[...] = jnp.zeros_like(bt)
    copies = sum_and_gather(
        here, first_block, take_first, part.at[0], held, own, relay.at[0],
        across.at[0], side.at[0], zpart.at[0], zgot.at[0], full.at[0], sems.at[0],
        lambda: pl.semaphore_wait(barrier, len(partners)),
    )

    for j in range(NP):
        bparts[j] = bt[:, j * K:(j + 1) * K].astype(BF16)
        total[j] = bt[:, j * K:(j + 1) * K]
    bs = {}
    for d in PIX_ORDER:
        bs[d] = send(bparts.at[(here.pix + d) % NP], bgot.at[d - 1], pix_sems.at[0], d - 1, here.at_pix(d))
    mine = total[here.pix]
    for d in range(1, NP):
        bs[d].wait_recv()
        mine = mine + bgot[d - 1].astype(F32)
    spot = back.at[rows(here.pix * K, K)]
    spot[...] = mine.T.astype(BF16)
    gs = [send(spot, spot, pix_sems.at[1], d - 1, here.at_pix(d)) for d in PIX_ORDER]
    for c in gs:
        c.wait_recv()
    copies += list(bs.values()) + gs

    def sketch_block(b):
        return jnp.dot(m[rows(b * BLOCK, BLOCK), :], back[...], preferred_element_type=F32)

    def take_sketch(b):
        where = rows(b * BLOCK, BLOCK)
        s = full[1, where, :]
        total[b] = contract(s, s, 0, 0)
        bt[...] += contract(s, m[where, :], 0, 0)

    bt[...] = jnp.zeros_like(bt)
    copies += sum_and_gather(
        here, sketch_block, take_sketch, part.at[1], held, own, relay.at[1],
        across.at[1], side.at[1], zpart.at[1], zgot.at[1], full.at[1], sems.at[1],
    )

    y, core = here.pix // 2, here.pix % 2
    near = (y * 2 + 1 - core, here.pos)
    mine_gram[...] = total[0] + total[1] + total[2] + total[3]
    keep, give = rows(core * HALF_K, HALF_K), rows((1 - core) * HALF_K, HALF_K)
    swap = send(mine_gram.at[give], half_got, gram_sems, 0, near)
    swap.wait_recv()
    halves[y] = mine_gram[keep, :] + half_got[...]
    spot = halves.at[y]
    ys = [send(spot, spot, gram_sems, d, ((y + d) % 4 * 2 + core, here.pos)) for d in (1, 2, 3)]
    for j in range(NP):
        pparts[j] = bt[:, j * K:(j + 1) * K].astype(BF16)
        total[j] = bt[:, j * K:(j + 1) * K]
    ps = {}
    for d in PIX_ORDER:
        ps[d] = send(pparts.at[(here.pix + d) % NP], pgot.at[d - 1], pix_sems.at[2], d - 1, here.at_pix(d))
    for c in copies:
        c.wait_send()
    for c in ys:
        c.wait_recv()
    gram[keep, :] = (halves[0] + halves[1]) + (halves[2] + halves[3])
    spot = gram.at[keep]
    swap_back = send(spot, spot, gram_sems, 4, near)
    mine = total[here.pix]
    for d in range(1, NP):
        ps[d].wait_recv()
        mine = mine + pgot[d - 1].astype(F32)
    pall[here.pix] = mine.astype(BF16)
    spot = pall.at[here.pix]
    gs = [send(spot, spot, pix_sems.at[3], d - 1, here.at_pix(d)) for d in PIX_ORDER]
    swap_back.wait_recv()
    copies = [swap, swap_back] + ys + list(ps.values()) + gs
    inverse = inverse_factor(gram[...])
    factor[...] = inverse

    scaled = inverse.T * SCALE
    top, mid, low = thirds(scaled)
    for b in range(NX):
        where = pl.ds(b * BLOCK, BLOCK)
        s = full[1, where, :]
        basis_out[where, :] = (
            jnp.dot(s, top, preferred_element_type=F32)
            + jnp.dot(s, mid, preferred_element_type=F32)
            + jnp.dot(s, low, preferred_element_type=F32)
        )
    share = K // NP
    lines = jnp.concatenate(thirds(factor[rows(here.pix * share, share), :]), axis=0)
    for c in gs:
        c.wait_recv()
    for j in range(NP):
        product = jnp.dot(lines, pall[j], preferred_element_type=F32)
        projected_out[:, j * K:(j + 1) * K] = product[:share] + product[share:2 * share] + product[2 * share:]
    for c in copies:
        c.wait_send()


def body(stack, omega):
    vmem = pl.BlockSpec(memory_space=pltpu.VMEM)
    hbm = pl.BlockSpec(memory_space=pl.ANY)
    basis, projected = pl.pallas_call(
        whole_kernel,
        out_shape=(
            jax.ShapeDtypeStruct((ROWS, K), F32),
            jax.ShapeDtypeStruct((K // NP, COLS), F32),
        ),
        in_specs=[hbm, pl.BlockSpec(memory_space=pltpu.HBM)],
        out_specs=(vmem, vmem),
        scratch_shapes=[
            pltpu.VMEM((ROWS, COLS), BF16),
            pltpu.VMEM((COLS, K), jnp.int32),
            pltpu.VMEM((COLS, K), BF16),
            pltpu.VMEM((2, 3, BLOCK, K), BF16),
            pltpu.VMEM((3, BLOCK, K), F32),
            pltpu.VMEM((BLOCK, K), F32),
            pltpu.VMEM((2, NZ, CHUNK, K), BF16),
            pltpu.VMEM((2, 3, NZ, CHUNK, K), BF16),
            pltpu.VMEM((2, 3, 2, CHUNK, K), BF16),
            pltpu.VMEM((2, NZ - 1, CHUNK, K), BF16),
            pltpu.VMEM((2, NZ - 1, CHUNK, K), BF16),
            pltpu.VMEM((2, ROWS, K), BF16),
            pltpu.VMEM((K, COLS), F32),
            pltpu.VMEM((NP, K, K), BF16),
            pltpu.VMEM((NP - 1, K, K), BF16),
            pltpu.VMEM((COLS, K), BF16),
            pltpu.VMEM((NP, K, K), F32),
            pltpu.VMEM((K, K), F32),
            pltpu.VMEM((HALF_K, K), F32),
            pltpu.VMEM((4, HALF_K, K), F32),
            pltpu.VMEM((K, K), F32),
            pltpu.VMEM((K, K), F32),
            pltpu.VMEM((NP, K, K), BF16),
            pltpu.VMEM((NP - 1, K, K), BF16),
            pltpu.VMEM((NP, K, K), BF16),
            pltpu.SemaphoreType.DMA((5,)),
            pltpu.SemaphoreType.DMA((2, 2, 10 * NZ)),
            pltpu.SemaphoreType.DMA((4, 2, NP - 1)),
            pltpu.SemaphoreType.DMA((2, 5)),
        ],
        compiler_params=pltpu.CompilerParams(
            collective_id=0, has_side_effects=True, vmem_limit_bytes=48 << 20
        ),
        cost_estimate=pl.CostEstimate(flops=4 * 2 * ROWS * COLS * K, bytes_accessed=12 << 20, transcendentals=0),
    )(stack, omega)
    return basis.reshape(stack.shape[0], 2, K), projected


def solution(mesh):
    return jax.shard_map(
        body,
        mesh=mesh,
        in_specs=(P("pix", None, "pos"), P("pos", None)),
        out_specs=(P("pix", None, None), P("pix", "pos")),
        check_vma=False,
    )
```
